32 devices in a mesh: groups: 2 (over y), row: 4 (over x, core), col: 4 (over z).
Axes of the slice: x: 2, y: 2, z: 4, core: 2. Of those that a mesh axis runs over, the one named last changes fastest.
Arguments:
- pair: bfloat16 [1024, 512, 128], P(('groups', 'row'), 'col'), parts along dimension 0, may hold values from -6 to 6
- token_mask: int32 [1024], P('groups'), parts along dimension 0, may hold values 0 or 1
- token_count: int32 [2], P('groups'), parts along dimension 0, may hold values from 256 to 512
- out_inputs: bfloat16 [128, 512], replicated, may hold values from -0.5 to 0.5
- out_gating: bfloat16 [128, 128], replicated, may hold values from -0.5 to 0.5
- out_final: bfloat16 [128, 128], replicated, may hold values from -0.5 to 0.5
- in_inputs: bfloat16 [128, 512], replicated, may hold values from -0.5 to 0.5
- in_gating: bfloat16 [128, 128], replicated, may hold values from -0.5 to 0.5
- in_final: bfloat16 [128, 128], replicated, may hold values from -0.5 to 0.5
Outputs:
- updated: bfloat16 [1024, 512, 128], P(('groups', 'row'), 'col'), parts along dimension 0
The draws below stay inside these ranges and needn't reach their ends.
There are 2 independent parts, one for each index of `groups`. The reference program is written for one: setup_inputs(seed, part) draws one part's arguments, and reference() takes and returns one part's arrays. A program takes and returns all parts, laid end to end along the dimension named above; an argument that names none is the same for every part. Nothing has to cross between parts.
Inputs may be any that keep to these rules, and one draw needn't show every extreme that they name: Token positions token_count and beyond are padding.
All inputs are finite; a program needn't handle non-finite values.
Results may differ from the reference program's by a relative error of at most 0.0054.
Values may be sent and summed in bfloat16 or wider, within the bound.
A program may use at most 192 MiB of HBM per device.

```python
import jax
import jax.numpy as jnp
from jax import lax

C = 128
H = 128
N = 512


def set_ends(result, stream_key, smallest, top_value):
    shape = result.shape
    index_at = [jax.random.randint(jax.random.fold_in(stream_key, axis), (), 0, shape[axis]) for axis in range(len(shape))]
    result = result.at[tuple(index_at)].set(smallest)
    longest = shape.index(max(shape))
    index_at[longest] = (index_at[longest] + 1) % shape[longest]
    return result.at[tuple(index_at)].set(top_value)


def levels(key, dims, split, least, largest):
    def one(position, shards_of):
        draws = jax.random.uniform(jax.random.fold_in(jax.random.fold_in(key, 6), position), (shards_of,), jnp.float32, least / len(split), largest / len(split))
        return jnp.repeat(jnp.exp(draws), dims[position] // shards_of).reshape((-1,) + (1,) * (len(dims) - position - 1))

    factor_of = one(*split[0])
    for cut in split[1:]:
        factor_of = factor_of * one(*cut)
    return factor_of


def normal_values(stream_key, shape, spread, reach, pieces=(), dtype=jnp.bfloat16):
    level = levels(stream_key, shape, pieces, -0.22, 0.18) if pieces else 1.0
    result = jax.random.normal(stream_key, shape, jnp.float32) * spread * level
    return jnp.minimum(jnp.maximum(result, -reach), reach).astype(dtype)


def setup_inputs(seed: int = 0, part: int = 0) -> dict:
    streams_of = jax.random.split(jax.random.key(seed), 10)
    part_splits = jax.random.split(jax.random.fold_in(streams_of[9], part), 10)
    pair = normal_values(part_splits[0], (N, N, C), 1.0, 6.0, ((0, 4), (1, 4)))
    token_mask = set_ends((jax.random.randint(part_splits[1], (N,), 0, 8) < 7).astype(jnp.int32), jax.random.fold_in(part_splits[1], 1), 0, 1)
    token_count = jax.random.randint(part_splits[2], (1,), N // 2, N + 1).astype(jnp.int32)
    out_inputs = normal_values(streams_of[3], (C, 4 * H), C ** -0.5, 0.5)
    out_gating = normal_values(streams_of[4], (C, C), C ** -0.5, 0.5)
    out_final = normal_values(streams_of[5], (H, C), H ** -0.5, 0.5)
    in_inputs = normal_values(streams_of[6], (C, 4 * H), C ** -0.5, 0.5)
    in_gating = normal_values(streams_of[7], (C, C), C ** -0.5, 0.5)
    in_final = normal_values(streams_of[8], (H, C), H ** -0.5, 0.5)
    return {"pair": pair, "token_mask": token_mask, "token_count": token_count, "out_inputs": out_inputs, "out_gating": out_gating, "out_final": out_final, "in_inputs": in_inputs, "in_gating": in_gating, "in_final": in_final}


def layer_norm(x):
    mean = lax.optimization_barrier(jnp.mean(x, axis=-1, keepdims=True))
    centred = x - mean
    var = lax.optimization_barrier(jnp.mean(centred * centred, axis=-1, keepdims=True))
    return centred * lax.rsqrt(var + 1e-05)

def prepare(field, pmask, w_inputs, w_gating):
    hidden = w_inputs.shape[1] // 4
    normed = layer_norm(field.astype(jnp.float32)).astype(jnp.bfloat16)
    flat = normed.reshape(-1, normed.shape[-1])
    proj = jnp.dot(flat, w_inputs, preferred_element_type=jnp.float32)
    proj = proj.reshape(field.shape[0], field.shape[1], 4 * hidden)
    left = (pmask[..., None] * jax.nn.sigmoid(proj[..., :hidden]) * proj[..., hidden:2 * hidden]).astype(jnp.bfloat16)
    right = (pmask[..., None] * jax.nn.sigmoid(proj[..., 2 * hidden:3 * hidden]) * proj[..., 3 * hidden:]).astype(jnp.bfloat16)
    gate = jax.nn.sigmoid(jnp.dot(flat, w_gating, preferred_element_type=jnp.float32))
    return (left, right, gate.reshape(field.shape[0], field.shape[1], -1))

def finish(field, tri, gate, w_final):
    tnorm = layer_norm(tri).astype(jnp.bfloat16)
    flat = tnorm.reshape(-1, tnorm.shape[-1])
    value = jnp.dot(flat, w_final, preferred_element_type=jnp.float32).reshape(gate.shape)
    return (field.astype(jnp.float32) + gate * value).astype(jnp.bfloat16)

def reference(pair, token_mask, token_count, out_inputs, out_gating, out_final, in_inputs, in_gating, in_final):
    positions = lax.iota(jnp.int32, token_mask.shape[0])
    valid = token_mask * (positions < token_count[0]).astype(jnp.int32)
    validf = valid.astype(jnp.float32)
    pmask = validf[:, None] * validf[None, :]
    left, right, gate = prepare(pair, pmask, out_inputs, out_gating)
    tri = jnp.einsum('ikh,jkh->ijh', left.astype(jnp.float32), right.astype(jnp.float32), precision=lax.Precision.HIGHEST)
    middle = finish(pair, tri, gate, out_final)
    left, right, gate = prepare(middle, pmask, in_inputs, in_gating)
    tri = jnp.einsum('kih,kjh->ijh', left.astype(jnp.float32), right.astype(jnp.float32), precision=lax.Precision.HIGHEST)
    return finish(middle, tri, gate, in_final)
```

```python
import functools

import jax
import jax.numpy as jnp
from jax import lax
from jax.experimental import pallas as pl
from jax.experimental.pallas import tpu as pltpu
from jax.sharding import PartitionSpec as P

AXES = ("row", "col")


def layer_norm(x, axis=-1):
    mean = jnp.mean(x, axis=axis, keepdims=True)
    centred = x - mean
    var = jnp.mean(centred * centred, axis=axis, keepdims=True)
    return centred * lax.rsqrt(var + 1e-05)


def product_kernel(rows, cols, outgoing, a_ref, b_ref, o_ref, a_full, b_full, t_full):
    height, width = a_ref.shape[-2:]
    for r in range(rows):
        for c in range(cols):
            at = (slice(r * height, (r + 1) * height), slice(c * width, (c + 1) * width))
            a_full[at] = a_ref[r * cols + c, 0]
            b_full[at] = b_ref[r * cols + c, 0]
    dims = (((1,), (1,)), ((), ())) if outgoing else (((0,), (0,)), ((), ()))
    t_full[...] = lax.dot_general(
        a_full[...], b_full[...], dims, preferred_element_type=jnp.float32
    ).astype(jnp.bfloat16)
    for r in range(rows):
        for c in range(cols):
            at = (slice(r * height, (r + 1) * height), slice(c * width, (c + 1) * width))
            o_ref[r * cols + c, 0] = t_full[at]


def product(a, b, rows, cols, outgoing):
    parts, hidden, height, width = a.shape
    n = rows * height
    spec = pl.BlockSpec((parts, 1, height, width), lambda h: (0, h, 0, 0))
    return pl.pallas_call(
        functools.partial(product_kernel, rows, cols, outgoing),
        grid=(hidden,),
        in_specs=[spec, spec],
        out_specs=spec,
        out_shape=jax.ShapeDtypeStruct(a.shape, jnp.bfloat16),
        scratch_shapes=[pltpu.VMEM((n, n), jnp.bfloat16)] * 3,
        compiler_params=pltpu.CompilerParams(vmem_limit_bytes=40 * 2**20),
        cost_estimate=pl.CostEstimate(
            flops=2 * hidden * n**3, bytes_accessed=6 * hidden * n * n, transcendentals=0
        ),
    )(a, b)


def exchange(x):
    return lax.all_to_all(x, AXES, 0, 0, tiled=True)


def update(field, pmask, w_inputs, w_gating, w_final, outgoing):
    rows, cols = lax.axis_size("row"), lax.axis_size("col")
    parts = rows * cols
    height, width = field.shape[:2]
    hidden = w_inputs.shape[1] // 4
    normed = layer_norm(field.astype(jnp.float32)).astype(jnp.bfloat16)

    def side(first):
        def one(start):
            w = w_inputs[:, start : start + hidden]
            return lax.dot_general(
                w, normed, (((0,), (2,)), ((), ())), preferred_element_type=jnp.float32
            )

        value = pmask[None] * jax.nn.sigmoid(one(first)) * one(first + hidden)
        return exchange(value.astype(jnp.bfloat16)).reshape(parts, -1, height, width)

    a = side(0)
    b = side(2 * hidden)
    gate = jax.nn.sigmoid(jnp.dot(normed, w_gating, preferred_element_type=jnp.float32))
    tri = product(a, b, rows, cols, outgoing)
    tri = exchange(tri.reshape(hidden, height, width)).astype(jnp.float32)
    tnorm = layer_norm(tri, 0).astype(jnp.bfloat16)
    value = lax.dot_general(
        tnorm, w_final, (((0,), (0,)), ((), ())), preferred_element_type=jnp.float32
    )
    return (field.astype(jnp.float32) + gate * value).astype(jnp.bfloat16)


def local(
    pair, token_mask, token_count, out_inputs, out_gating, out_final, in_inputs, in_gating, in_final
):
    height, width = pair.shape[:2]
    positions = lax.iota(jnp.int32, token_mask.shape[0])
    valid = (token_mask * (positions < token_count[0]).astype(jnp.int32)).astype(jnp.float32)
    row_valid = lax.dynamic_slice_in_dim(valid, lax.axis_index("row") * height, height)
    col_valid = lax.dynamic_slice_in_dim(valid, lax.axis_index("col") * width, width)
    pmask = row_valid[:, None] * col_valid[None, :]
    middle = update(pair, pmask, out_inputs, out_gating, out_final, True)
    return update(middle, pmask, in_inputs, in_gating, in_final, False)


def solution(mesh):
    tile = P(("groups", "row"), "col", None)
    in_specs = (tile, P("groups"), P("groups")) + (P(),) * 6
    return jax.shard_map(local, mesh=mesh, in_specs=in_specs, out_specs=tile, check_vma=False)
```

```python
import functools

import jax
import jax.numpy as jnp
from jax import lax
from jax.experimental import pallas as pl
from jax.experimental.pallas import tpu as pltpu
from jax.sharding import PartitionSpec as P

CHUNKS = 4


def layer_norm(x, axis=-1):
    mean = jnp.mean(x, axis=axis, keepdims=True)
    centred = x - mean
    var = jnp.mean(centred * centred, axis=axis, keepdims=True)
    return centred * lax.rsqrt(var + 1e-05)


MESH = pl.DeviceIdType.MESH


def triangle_kernel(
    outgoing, chunks, rows, half_cols, a_hbm, b_hbm, o_hbm, a_in, b_in, t_out, a_full, b_full,
    a_send, a_recv, b_send, b_recv, t_send, t_recv, own_sem,
):
    members = rows * half_cols
    depth = a_in.shape[3]
    owned = depth * chunks
    height, width = a_in.shape[-2:]
    row, col = lax.axis_index("row"), lax.axis_index("col")
    half = lax.div(col, half_cols)
    mine = row * half_cols + lax.rem(col, half_cols)
    a_flips = 1 if outgoing else 2
    t_flips = 2 if outgoing else 1

    def side_of(flip):
        return half if flip == 0 else 1 - half

    def ahead(off):
        return lax.rem(mine + off, members)

    def behind(off):
        return lax.rem(mine + members - off, members)

    def place(flip, member):
        return {
            "row": lax.div(member, half_cols),
            "col": side_of(flip) * half_cols + lax.rem(member, half_cols),
        }

    def slots(count, flip):
        return side_of(flip) if count == 2 else 0

    def each(flips, body):
        for flip in reversed(range(flips)):
            first = 1 if flip == 0 else 0

            def one(off, carry, flip=flip):
                body(flip, off)
                return carry

            lax.fori_loop(first, members, one, 0)

    def inward(source, landing, send, recv, flips, q, flip, off, slot_side, slot_member):
        target = ahead(off)
        return pltpu.make_async_remote_copy(
            src_ref=source.at[pl.ds(target * owned + q * depth, depth)],
            dst_ref=landing.at[q, slot_side, slot_member],
            send_sem=send.at[q, flip, off],
            recv_sem=recv.at[q, flip, off],
            device_id=place(flip, target),
            device_id_type=MESH,
        )

    def outward(q, flip, off, o_side, o_member):
        target = ahead(off)
        return pltpu.make_async_remote_copy(
            src_ref=t_out.at[q, slots(t_flips, flip), target],
            dst_ref=o_hbm.at[o_side, pl.ds(o_member * owned + q * depth, depth)],
            send_sem=t_send.at[q, flip, off],
            recv_sem=t_recv.at[q, flip, off],
            device_id=place(flip, target),
            device_id_type=MESH,
        )

    operands = (
        (a_hbm, a_in, a_send, a_recv, a_flips),
        (b_hbm, b_in, b_send, b_recv, 1),
    )

    def local_in(which, q):
        source, landing, _, _, flips = operands[which]
        return pltpu.make_async_copy(
            source.at[pl.ds(mine * owned + q * depth, depth)],
            landing.at[q, slots(flips, 0), mine],
            own_sem.at[which, q],
        )

    def local_out(q):
        return pltpu.make_async_copy(
            t_out.at[q, slots(t_flips, 0), mine],
            o_hbm.at[slots(t_flips, 0), pl.ds(mine * owned + q * depth, depth)],
            own_sem.at[2, q],
        )

    def start_in(q):
        for which in range(2):
            source, landing, send, recv, flips = operands[which]
            each(
                flips,
                lambda flip, off: inward(
                    source, landing, send, recv, flips, q, flip, off, slots(flips, 0), mine
                ).start(),
            )
            local_in(which, q).start()

    def wait_in(q):
        for which in range(2):
            source, landing, send, recv, flips = operands[which]
            each(
                flips,
                lambda flip, off: inward(
                    source, landing, send, recv, flips, q, flip, off, slots(flips, flip), behind(off)
                ).wait_recv(),
            )
            local_in(which, q).wait()

    barrier = pltpu.get_barrier_semaphore()
    each(
        2,
        lambda flip, off: pl.semaphore_signal(
            barrier, inc=1, device_id=place(flip, ahead(off)), device_id_type=MESH
        ),
    )
    pl.semaphore_wait(barrier, 2 * members - 1)

    def fill(full, landing, q, channel, flips):
        for side in range(flips):
            for member in range(members):
                r = (member // half_cols) * height
                c = (side * half_cols + member % half_cols) * width
                full[r : r + height, c : c + width] = landing[q, side, member, channel]

    dims = (((1,), (1,)), ((), ())) if outgoing else (((0,), (0,)), ((), ()))

    ready = min(2, chunks)
    for q in range(ready):
        start_in(q)
    for q in range(chunks):
        wait_in(q)

        def multiply(channel, carry, q=q):
            fill(a_full, a_in, q, channel, a_flips)
            fill(b_full, b_in, q, channel, 1)
            tri = lax.dot_general(
                a_full[...], b_full[...], dims, preferred_element_type=jnp.float32
            ).astype(jnp.bfloat16)
            for side in range(t_flips):
                for member in range(members):
                    r = (member // half_cols) * height
                    c = (side * half_cols + member % half_cols) * width
                    t_out[q, side, member, channel] = tri[r : r + height, c : c + width]
            return carry

        lax.fori_loop(0, depth, multiply, 0)
        each(
            t_flips, lambda flip, off: outward(q, flip, off, slots(t_flips, 0), mine).start()
        )
        local_out(q).start()
        if q + ready < chunks:
            start_in(q + ready)
    for q in range(chunks):
        for which in range(2):
            source, landing, send, recv, flips = operands[which]
            each(
                flips,
                lambda flip, off: inward(
                    source, landing, send, recv, flips, q, flip, off, slots(flips, 0), mine
                ).wait_send(),
            )
        each(
            t_flips, lambda flip, off: outward(q, flip, off, slots(t_flips, 0), mine).wait_send()
        )
        each(
            t_flips,
            lambda flip, off: outward(q, flip, off, slots(t_flips, flip), behind(off)).wait_recv(),
        )
        local_out(q).wait()


def triangle(a, b, rows, cols, outgoing):
    hidden, height, width = a.shape
    half_cols = cols // 2
    members = rows * half_cols
    owned = hidden // members
    chunks = min(CHUNKS, owned)
    depth = owned // chunks
    n = rows * height
    a_flips, t_flips = (1, 2) if outgoing else (2, 1)

    def blocks(flips):
        return pltpu.VMEM((chunks, flips, members, depth, height, width), jnp.bfloat16)

    def sems(flips):
        return pltpu.SemaphoreType.DMA((chunks, flips, members))

    anywhere = pl.BlockSpec(memory_space=pl.ANY)
    return pl.pallas_call(
        functools.partial(triangle_kernel, outgoing, chunks, rows, half_cols),
        in_specs=[anywhere, anywhere],
        out_specs=anywhere,
        out_shape=jax.ShapeDtypeStruct((t_flips, hidden, height, width), jnp.bfloat16),
        scratch_shapes=[
            blocks(a_flips),
            blocks(1),
            blocks(t_flips),
            pltpu.VMEM((n, a_flips * half_cols * width), jnp.bfloat16),
            pltpu.VMEM((n, half_cols * width), jnp.bfloat16),
            sems(a_flips),
            sems(a_flips),
            sems(1),
            sems(1),
            sems(t_flips),
            sems(t_flips),
            pltpu.SemaphoreType.DMA((3, chunks)),
        ],
        compiler_params=pltpu.CompilerParams(
            collective_id=0 if outgoing else 1,
            has_side_effects=True,
            vmem_limit_bytes=48 * 2**20,
        ),
    )(a, b)


def update(field, pmask, w_inputs, w_gating, w_final, outgoing):
    rows, cols = lax.axis_size("row"), lax.axis_size("col")
    hidden = w_inputs.shape[1] // 4
    normed = layer_norm(field.astype(jnp.float32)).astype(jnp.bfloat16)

    def side(first):
        def one(start):
            w = w_inputs[:, start : start + hidden]
            return lax.dot_general(
                w, normed, (((0,), (2,)), ((), ())), preferred_element_type=jnp.float32
            )

        value = pmask[None] * jax.nn.sigmoid(one(first)) * one(first + hidden)
        return value.astype(jnp.bfloat16)

    a = side(0)
    b = side(2 * hidden)
    gate = jax.nn.sigmoid(jnp.dot(normed, w_gating, preferred_element_type=jnp.float32))
    tri = jnp.sum(triangle(a, b, rows, cols, outgoing).astype(jnp.float32), 0)
    tnorm = layer_norm(tri, 0).astype(jnp.bfloat16)
    value = lax.dot_general(
        tnorm, w_final, (((0,), (0,)), ((), ())), preferred_element_type=jnp.float32
    )
    return (field.astype(jnp.float32) + gate * value).astype(jnp.bfloat16)


def local(
    pair, token_mask, token_count, out_inputs, out_gating, out_final, in_inputs, in_gating, in_final
):
    height, width = pair.shape[:2]
    positions = lax.iota(jnp.int32, token_mask.shape[0])
    valid = (token_mask * (positions < token_count[0]).astype(jnp.int32)).astype(jnp.float32)
    row_valid = lax.dynamic_slice_in_dim(valid, lax.axis_index("row") * height, height)
    col_valid = lax.dynamic_slice_in_dim(valid, lax.axis_index("col") * width, width)
    pmask = row_valid[:, None] * col_valid[None, :]
    middle = update(pair, pmask, out_inputs, out_gating, out_final, True)
    return update(middle, pmask, in_inputs, in_gating, in_final, False)


def solution(mesh):
    tile = P(("groups", "row"), "col", None)
    in_specs = (tile, P("groups"), P("groups")) + (P(),) * 6
    return jax.shard_map(local, mesh=mesh, in_specs=in_specs, out_specs=tile, check_vma=False)
```

```python
import functools

import jax
import jax.numpy as jnp
from jax import lax
from jax.experimental import pallas as pl
from jax.experimental.pallas import tpu as pltpu
from jax.sharding import PartitionSpec as P

CHUNKS = 4


MESH = pl.DeviceIdType.MESH


def triangle_kernel(
    outgoing, chunks, rows, half_cols, a_hbm, b_hbm, o_hbm, a_in, b_in, t_out, a_full, b_full,
    a_send, a_recv, b_send, b_recv, t_send, t_recv, own_sem,
):
    members = rows * half_cols
    depth = a_in.shape[3]
    owned = depth * chunks
    height, width = a_in.shape[-2:]
    row, col = lax.axis_index("row"), lax.axis_index("col")
    half = lax.div(col, half_cols)
    mine = row * half_cols + lax.rem(col, half_cols)
    a_flips = 1 if outgoing else 2
    t_flips = 2 if outgoing else 1

    def side_of(flip):
        return half if flip == 0 else 1 - half

    def ahead(off):
        return lax.rem(mine + off, members)

    def behind(off):
        return lax.rem(mine + members - off, members)

    def place(flip, member):
        return {
            "row": lax.div(member, half_cols),
            "col": side_of(flip) * half_cols + lax.rem(member, half_cols),
        }

    def slots(count, flip):
        return side_of(flip) if count == 2 else 0

    def each(flips, body):
        for flip in reversed(range(flips)):
            first = 1 if flip == 0 else 0

            def one(off, carry, flip=flip):
                body(flip, off)
                return carry

            lax.fori_loop(first, members, one, 0)

    def inward(source, landing, send, recv, flips, q, flip, off, slot_side, slot_member):
        target = ahead(off)
        return pltpu.make_async_remote_copy(
            src_ref=source.at[pl.ds(target * owned + q * depth, depth)],
            dst_ref=landing.at[q, slot_side, slot_member],
            send_sem=send.at[q, flip, off],
            recv_sem=recv.at[q, flip, off],
            device_id=place(flip, target),
            device_id_type=MESH,
        )

    def outward(q, flip, off, o_side, o_member):
        target = ahead(off)
        return pltpu.make_async_remote_copy(
            src_ref=t_out.at[q, slots(t_flips, flip), target],
            dst_ref=o_hbm.at[o_side, pl.ds(o_member * owned + q * depth, depth)],
            send_sem=t_send.at[q, flip, off],
            recv_sem=t_recv.at[q, flip, off],
            device_id=place(flip, target),
            device_id_type=MESH,
        )

    operands = (
        (a_hbm, a_in, a_send, a_recv, a_flips),
        (b_hbm, b_in, b_send, b_recv, 1),
    )

    def local_in(which, q):
        source, landing, _, _, flips = operands[which]
        return pltpu.make_async_copy(
            source.at[pl.ds(mine * owned + q * depth, depth)],
            landing.at[q, slots(flips, 0), mine],
            own_sem.at[which, q],
        )

    def local_out(q):
        return pltpu.make_async_copy(
            t_out.at[q, slots(t_flips, 0), mine],
            o_hbm.at[slots(t_flips, 0), pl.ds(mine * owned + q * depth, depth)],
            own_sem.at[2, q],
        )

    def start_in(q):
        for which in range(2):
            source, landing, send, recv, flips = operands[which]
            each(
                flips,
                lambda flip, off: inward(
                    source, landing, send, recv, flips, q, flip, off, slots(flips, 0), mine
                ).start(),
            )
            local_in(which, q).start()

    def wait_in(q):
        for which in range(2):
            source, landing, send, recv, flips = operands[which]
            each(
                flips,
                lambda flip, off: inward(
                    source, landing, send, recv, flips, q, flip, off, slots(flips, flip), behind(off)
                ).wait_recv(),
            )
            local_in(which, q).wait()

    barrier = pltpu.get_barrier_semaphore()
    each(
        2,
        lambda flip, off: pl.semaphore_signal(
            barrier, inc=1, device_id=place(flip, ahead(off)), device_id_type=MESH
        ),
    )
    pl.semaphore_wait(barrier, 2 * members - 1)

    def fill(full, landing, q, channel, flips):
        for side in range(flips):
            for member in range(members):
                r = (member // half_cols) * height
                c = (side * half_cols + member % half_cols) * width
                full[r : r + height, c : c + width] = landing[q, side, member, channel]

    dims = (((1,), (1,)), ((), ())) if outgoing else (((0,), (0,)), ((), ()))

    ready = min(2, chunks)
    for q in range(ready):
        start_in(q)
    for q in range(chunks):
        wait_in(q)

        def multiply(channel, carry, q=q):
            fill(a_full, a_in, q, channel, a_flips)
            fill(b_full, b_in, q, channel, 1)
            tri = lax.dot_general(
                a_full[...], b_full[...], dims, preferred_element_type=jnp.float32
            ).astype(jnp.bfloat16)
            for side in range(t_flips):
                for member in range(members):
                    r = (member // half_cols) * height
                    c = (side * half_cols + member % half_cols) * width
                    t_out[q, side, member, channel] = tri[r : r + height, c : c + width]
            return carry

        lax.fori_loop(0, depth, multiply, 0)
        each(
            t_flips, lambda flip, off: outward(q, flip, off, slots(t_flips, 0), mine).start()
        )
        local_out(q).start()
        if q + ready < chunks:
            start_in(q + ready)
    for q in range(chunks):
        for which in range(2):
            source, landing, send, recv, flips = operands[which]
            each(
                flips,
                lambda flip, off: inward(
                    source, landing, send, recv, flips, q, flip, off, slots(flips, 0), mine
                ).wait_send(),
            )
        each(
            t_flips, lambda flip, off: outward(q, flip, off, slots(t_flips, 0), mine).wait_send()
        )
        each(
            t_flips,
            lambda flip, off: outward(q, flip, off, slots(t_flips, flip), behind(off)).wait_recv(),
        )
        local_out(q).wait()


def triangle(a, b, rows, cols, outgoing):
    hidden, height, width = a.shape
    half_cols = cols // 2
    members = rows * half_cols
    owned = hidden // members
    chunks = min(CHUNKS, owned)
    depth = owned // chunks
    n = rows * height
    a_flips, t_flips = (1, 2) if outgoing else (2, 1)

    def blocks(flips):
        return pltpu.VMEM((chunks, flips, members, depth, height, width), jnp.bfloat16)

    def sems(flips):
        return pltpu.SemaphoreType.DMA((chunks, flips, members))

    anywhere = pl.BlockSpec(memory_space=pl.ANY)
    return pl.pallas_call(
        functools.partial(triangle_kernel, outgoing, chunks, rows, half_cols),
        in_specs=[anywhere, anywhere],
        out_specs=anywhere,
        out_shape=jax.ShapeDtypeStruct((t_flips, hidden, height, width), jnp.bfloat16),
        scratch_shapes=[
            blocks(a_flips),
            blocks(1),
            blocks(t_flips),
            pltpu.VMEM((n, a_flips * half_cols * width), jnp.bfloat16),
            pltpu.VMEM((n, half_cols * width), jnp.bfloat16),
            sems(a_flips),
            sems(a_flips),
            sems(1),
            sems(1),
            sems(t_flips),
            sems(t_flips),
            pltpu.SemaphoreType.DMA((3, chunks)),
        ],
        compiler_params=pltpu.CompilerParams(
            collective_id=0 if outgoing else 1,
            has_side_effects=True,
            vmem_limit_bytes=48 * 2**20,
        ),
    )(a, b)


def layer_norm(x, axis):
    mean = jnp.mean(x, axis=axis, keepdims=True)
    centred = x - mean
    var = jnp.mean(centred * centred, axis=axis, keepdims=True)
    return centred * lax.rsqrt(var + 1e-05)


def sigmoid(x):
    return 0.5 * jnp.tanh(0.5 * x) + 0.5


def point_kernel(finishes, prepares, *refs):
    refs = list(refs)
    field_ref = refs.pop(0)
    height, width, channels = field_ref.shape
    if finishes:
        tri_ref, gate_ref, final_ref = refs.pop(0), refs.pop(0), refs.pop(0)
    if prepares:
        mask_ref, inputs_ref, gating_ref = refs.pop(0), refs.pop(0), refs.pop(0)
    if finishes:
        middle_ref = refs.pop(0)
    if prepares:
        a_ref, b_ref, new_gate_ref = refs.pop(0), refs.pop(0), refs.pop(0)
    one, two = refs

    if finishes:
        hidden = tri_ref.shape[1]
        tri = jnp.sum(tri_ref[...].astype(jnp.float32), 0)
        tnorm = layer_norm(tri, 0)
        for h in range(hidden):
            one[pl.ds(h, height, stride=hidden), :] = tnorm[h]

    def line(i, carry):
        field = field_ref[i].astype(jnp.float32)
        if finishes:
            at = pl.ds(pl.multiple_of(i * hidden, hidden), hidden)
            value = lax.dot_general(
                one[at, :].astype(jnp.bfloat16),
                final_ref[...],
                (((0,), (0,)), ((), ())),
                preferred_element_type=jnp.float32,
            )
            rounded = (field + gate_ref[i] * value).astype(jnp.bfloat16)
            middle_ref[i] = rounded
            field = rounded.astype(jnp.float32)
        if prepares:
            size = inputs_ref.shape[0] // 4
            normed = layer_norm(field, -1).astype(jnp.bfloat16)
            proj = lax.dot_general(
                inputs_ref[...], normed, (((1,), (1,)), ((), ())),
                preferred_element_type=jnp.float32,
            )
            mask = mask_ref[pl.ds(i, 1), :]
            at = pl.ds(pl.multiple_of(i * size, size), size)
            one[at, :] = mask * sigmoid(proj[:size]) * proj[size : 2 * size]
            two[at, :] = mask * sigmoid(proj[2 * size : 3 * size]) * proj[3 * size :]
            new_gate_ref[i] = sigmoid(
                jnp.dot(normed, gating_ref[...], preferred_element_type=jnp.float32)
            )
        return carry

    lax.fori_loop(0, height, line, 0, unroll=4)
    if prepares:
        hidden = a_ref.shape[0]
        for h in range(hidden):
            rows = pl.ds(h, height, stride=hidden)
            a_ref[h] = one[rows, :].astype(jnp.bfloat16)
            b_ref[h] = two[rows, :].astype(jnp.bfloat16)


def point(field, finish=None, prepare=None):
    rows, width, channels = field.shape
    block = 16
    line_spec = pl.BlockSpec((block, width, channels), lambda i: (i, 0, 0))
    args, in_specs, outs, out_specs = [field], [line_spec], [], []

    def whole(array):
        args.append(array)
        in_specs.append(pl.BlockSpec(array.shape, lambda i: (0,) * array.ndim))

    if finish is not None:
        tri, gate, final = finish
        hidden = tri.shape[1]
        args.extend((tri, gate))
        in_specs.append(
            pl.BlockSpec((tri.shape[0], hidden, block, width), lambda i: (0, 0, i, 0))
        )
        in_specs.append(line_spec)
        whole(final)
        outs.append(jax.ShapeDtypeStruct(field.shape, jnp.bfloat16))
        out_specs.append(line_spec)
    if prepare is not None:
        mask, inputs, gating = prepare
        hidden = inputs.shape[1] // 4
        args.append(mask)
        in_specs.append(pl.BlockSpec((block, width), lambda i: (i, 0)))
        whole(inputs.T)
        whole(gating)
        outs.extend([jax.ShapeDtypeStruct((hidden, rows, width), jnp.bfloat16)] * 2)
        out_specs.extend([pl.BlockSpec((hidden, block, width), lambda i: (0, i, 0))] * 2)
        outs.append(jax.ShapeDtypeStruct(field.shape, jnp.float32))
        out_specs.append(line_spec)
    return pl.pallas_call(
        functools.partial(point_kernel, finish is not None, prepare is not None),
        grid=(rows // block,),
        in_specs=in_specs,
        out_specs=out_specs,
        out_shape=outs,
        scratch_shapes=[pltpu.VMEM((block * hidden, width), jnp.float32)] * 2,
        compiler_params=pltpu.CompilerParams(vmem_limit_bytes=40 * 2**20),
    )(*args)


def local(
    pair, token_mask, token_count, out_inputs, out_gating, out_final, in_inputs, in_gating, in_final
):
    height, width = pair.shape[:2]
    sizes = lax.axis_size("row"), lax.axis_size("col")
    positions = lax.iota(jnp.int32, token_mask.shape[0])
    valid = (token_mask * (positions < token_count[0]).astype(jnp.int32)).astype(jnp.float32)
    row_valid = lax.dynamic_slice_in_dim(valid, lax.axis_index("row") * height, height)
    col_valid = lax.dynamic_slice_in_dim(valid, lax.axis_index("col") * width, width)
    pmask = row_valid[:, None] * col_valid[None, :]
    a, b, gate = point(pair, prepare=(pmask, out_inputs, out_gating))
    tri = triangle(a, b, *sizes, True)
    middle, a, b, gate = point(pair, (tri, gate, out_final), (pmask, in_inputs, in_gating))
    tri = triangle(a, b, *sizes, False)
    return point(middle, finish=(tri, gate, in_final))[0]


def solution(mesh):
    tile = P(("groups", "row"), "col", None)
    in_specs = (tile, P("groups"), P("groups")) + (P(),) * 6
    return jax.shard_map(local, mesh=mesh, in_specs=in_specs, out_specs=tile, check_vma=False)
```

```python
import functools

import jax
import jax.numpy as jnp
from jax import lax
from jax.experimental import pallas as pl
from jax.experimental.pallas import tpu as pltpu
from jax.sharding import PartitionSpec as P

CHUNKS = 4


MESH = pl.DeviceIdType.MESH


def triangle_kernel(
    outgoing, chunks, rows, half_cols, a_hbm, b_hbm, o_hbm, a_in, b_in, t_out, a_full, b_full,
    a_send, a_recv, b_send, b_recv, t_send, t_recv, own_sem,
):
    members = rows * half_cols
    depth = a_in.shape[3]
    owned = depth * chunks
    height, width = a_in.shape[-2:]
    row, col = lax.axis_index("row"), lax.axis_index("col")
    half = lax.div(col, half_cols)
    mine = row * half_cols + lax.rem(col, half_cols)
    a_flips = 1 if outgoing else 2
    t_flips = 2 if outgoing else 1

    def side_of(flip):
        return half if flip == 0 else 1 - half

    def ahead(off):
        return lax.rem(mine + off, members)

    def behind(off):
        return lax.rem(mine + members - off, members)

    def place(flip, member):
        return {
            "row": lax.div(member, half_cols),
            "col": side_of(flip) * half_cols + lax.rem(member, half_cols),
        }

    def slots(count, flip):
        return side_of(flip) if count == 2 else 0

    def each(flips, body):
        for flip in reversed(range(flips)):
            first = 1 if flip == 0 else 0

            def one(off, carry, flip=flip):
                body(flip, off)
                return carry

            lax.fori_loop(first, members, one, 0)

    def inward(source, landing, send, recv, flips, q, flip, off, slot_side, slot_member):
        target = ahead(off)
        return pltpu.make_async_remote_copy(
            src_ref=source.at[pl.ds(target * owned + q * depth, depth)],
            dst_ref=landing.at[q, slot_side, slot_member],
            send_sem=send.at[q, flip, off],
            recv_sem=recv.at[q, flip, off],
            device_id=place(flip, target),
            device_id_type=MESH,
        )

    def outward(q, flip, off, o_side, o_member):
        target = ahead(off)
        return pltpu.make_async_remote_copy(
            src_ref=t_out.at[q, slots(t_flips, flip), target],
            dst_ref=o_hbm.at[o_side, pl.ds(o_member * owned + q * depth, depth)],
            send_sem=t_send.at[q, flip, off],
            recv_sem=t_recv.at[q, flip, off],
            device_id=place(flip, target),
            device_id_type=MESH,
        )

    operands = (
        (a_hbm, a_in, a_send, a_recv, a_flips),
        (b_hbm, b_in, b_send, b_recv, 1),
    )

    def local_in(which, q):
        source, landing, _, _, flips = operands[which]
        return pltpu.make_async_copy(
            source.at[pl.ds(mine * owned + q * depth, depth)],
            landing.at[q, slots(flips, 0), mine],
            own_sem.at[which, q],
        )

    def local_out(q):
        return pltpu.make_async_copy(
            t_out.at[q, slots(t_flips, 0), mine],
            o_hbm.at[slots(t_flips, 0), pl.ds(mine * owned + q * depth, depth)],
            own_sem.at[2, q],
        )

    def start_in(q):
        for which in range(2):
            source, landing, send, recv, flips = operands[which]
            each(
                flips,
                lambda flip, off: inward(
                    source, landing, send, recv, flips, q, flip, off, slots(flips, 0), mine
                ).start(),
            )
            local_in(which, q).start()

    def wait_in(q):
        for which in range(2):
            source, landing, send, recv, flips = operands[which]
            each(
                flips,
                lambda flip, off: inward(
                    source, landing, send, recv, flips, q, flip, off, slots(flips, flip), behind(off)
                ).wait_recv(),
            )
            local_in(which, q).wait()

    barrier = pltpu.get_barrier_semaphore()
    each(
        2,
        lambda flip, off: pl.semaphore_signal(
            barrier, inc=1, device_id=place(flip, ahead(off)), device_id_type=MESH
        ),
    )
    pl.semaphore_wait(barrier, 2 * members - 1)

    def fill(full, landing, q, channel, flips):
        for side in range(flips):
            for member in range(members):
                r = (member // half_cols) * height
                c = (side * half_cols + member % half_cols) * width
                full[r : r + height, c : c + width] = landing[q, side, member, channel]

    dims = (((1,), (1,)), ((), ())) if outgoing else (((0,), (0,)), ((), ()))

    ready = min(2, chunks)
    for q in range(ready):
        start_in(q)
    for q in range(chunks):
        wait_in(q)

        def multiply(channel, carry, q=q):
            fill(a_full, a_in, q, channel, a_flips)
            fill(b_full, b_in, q, channel, 1)
            tri = lax.dot_general(
                a_full[...], b_full[...], dims, preferred_element_type=jnp.float32
            ).astype(jnp.bfloat16)
            for side in range(t_flips):
                for member in range(members):
                    r = (member // half_cols) * height
                    c = (side * half_cols + member % half_cols) * width
                    t_out[q, side, member, channel] = tri[r : r + height, c : c + width]
            return carry

        lax.fori_loop(0, depth, multiply, 0)
        each(
            t_flips, lambda flip, off: outward(q, flip, off, slots(t_flips, 0), mine).start()
        )
        local_out(q).start()
        if q + ready < chunks:
            start_in(q + ready)
    for q in range(chunks):
        for which in range(2):
            source, landing, send, recv, flips = operands[which]
            each(
                flips,
                lambda flip, off: inward(
                    source, landing, send, recv, flips, q, flip, off, slots(flips, 0), mine
                ).wait_send(),
            )
        each(
            t_flips, lambda flip, off: outward(q, flip, off, slots(t_flips, 0), mine).wait_send()
        )
        each(
            t_flips,
            lambda flip, off: outward(q, flip, off, slots(t_flips, flip), behind(off)).wait_recv(),
        )
        local_out(q).wait()


def triangle(a, b, rows, cols, outgoing):
    hidden, height, width = a.shape
    half_cols = cols // 2
    members = rows * half_cols
    owned = hidden // members
    chunks = min(CHUNKS, owned)
    depth = owned // chunks
    n = rows * height
    a_flips, t_flips = (1, 2) if outgoing else (2, 1)

    def blocks(flips):
        return pltpu.VMEM((chunks, flips, members, depth, height, width), jnp.bfloat16)

    def sems(flips):
        return pltpu.SemaphoreType.DMA((chunks, flips, members))

    anywhere = pl.BlockSpec(memory_space=pl.ANY)
    return pl.pallas_call(
        functools.partial(triangle_kernel, outgoing, chunks, rows, half_cols),
        in_specs=[anywhere, anywhere],
        out_specs=anywhere,
        out_shape=jax.ShapeDtypeStruct((t_flips, hidden, height, width), jnp.bfloat16),
        scratch_shapes=[
            blocks(a_flips),
            blocks(1),
            blocks(t_flips),
            pltpu.VMEM((n, a_flips * half_cols * width), jnp.bfloat16),
            pltpu.VMEM((n, half_cols * width), jnp.bfloat16),
            sems(a_flips),
            sems(a_flips),
            sems(1),
            sems(1),
            sems(t_flips),
            sems(t_flips),
            pltpu.SemaphoreType.DMA((3, chunks)),
        ],
        compiler_params=pltpu.CompilerParams(
            collective_id=0 if outgoing else 1,
            has_side_effects=True,
            vmem_limit_bytes=48 * 2**20,
        ),
    )(a, b)


def layer_norm(x, axis):
    mean = jnp.mean(x, axis=axis, keepdims=True)
    centred = x - mean
    var = jnp.mean(centred * centred, axis=axis, keepdims=True)
    return centred * lax.rsqrt(var + 1e-05)


def sigmoid(x):
    return 0.5 * jnp.tanh(0.5 * x) + 0.5


def point_kernel(finishes, prepares, *refs):
    refs = list(refs)
    field_ref = refs.pop(0)
    height, width, channels = field_ref.shape
    if finishes:
        tri_ref, gate_ref, final_ref = refs.pop(0), refs.pop(0), refs.pop(0)
    if prepares:
        mask_ref, inputs_ref, gating_ref = refs.pop(0), refs.pop(0), refs.pop(0)
    if finishes:
        middle_ref = refs.pop(0)
    if prepares:
        a_ref, b_ref, new_gate_ref = refs.pop(0), refs.pop(0), refs.pop(0)
    one, two = refs

    if finishes:
        hidden = tri_ref.shape[1]
        for h in range(hidden):
            tri = tri_ref[0, h].astype(jnp.float32)
            for side in range(1, tri_ref.shape[0]):
                tri = tri + tri_ref[side, h].astype(jnp.float32)
            one[pl.ds(h, height, stride=hidden), :] = tri

    def line(i):
        field = field_ref[i].astype(jnp.float32)
        if finishes:
            at = slice(i * hidden, (i + 1) * hidden)
            value = lax.dot_general(
                layer_norm(one[at, :], 0).astype(jnp.bfloat16),
                final_ref[...],
                (((0,), (0,)), ((), ())),
                preferred_element_type=jnp.float32,
            )
            rounded = (field + gate_ref[i] * value).astype(jnp.bfloat16)
            middle_ref[i] = rounded
            field = rounded.astype(jnp.float32)
        if prepares:
            size = inputs_ref.shape[0] // 4
            normed = layer_norm(field, -1).astype(jnp.bfloat16)
            proj = lax.dot_general(
                inputs_ref[...], normed, (((1,), (1,)), ((), ())),
                preferred_element_type=jnp.float32,
            )
            mask = mask_ref[i : i + 1, :]
            at = slice(i * size, (i + 1) * size)
            one[at, :] = mask * sigmoid(proj[:size]) * proj[size : 2 * size]
            two[at, :] = mask * sigmoid(proj[2 * size : 3 * size]) * proj[3 * size :]
            new_gate_ref[i] = sigmoid(
                jnp.dot(normed, gating_ref[...], preferred_element_type=jnp.float32)
            )

    for i in range(height):
        line(i)
    if prepares:
        hidden = a_ref.shape[0]
        for h in range(hidden):
            rows = pl.ds(h, height, stride=hidden)
            a_ref[h] = one[rows, :].astype(jnp.bfloat16)
            b_ref[h] = two[rows, :].astype(jnp.bfloat16)


def point(field, finish=None, prepare=None):
    rows, width, channels = field.shape
    block = 16
    line_spec = pl.BlockSpec((block, width, channels), lambda i: (i, 0, 0))
    args, in_specs, outs, out_specs = [field], [line_spec], [], []

    def whole(array):
        args.append(array)
        in_specs.append(pl.BlockSpec(array.shape, lambda i: (0,) * array.ndim))

    if finish is not None:
        tri, gate, final = finish
        hidden = tri.shape[1]
        args.extend((tri, gate))
        in_specs.append(
            pl.BlockSpec((tri.shape[0], hidden, block, width), lambda i: (0, 0, i, 0))
        )
        in_specs.append(line_spec)
        whole(final)
        outs.append(jax.ShapeDtypeStruct(field.shape, jnp.bfloat16))
        out_specs.append(line_spec)
    if prepare is not None:
        mask, inputs, gating = prepare
        hidden = inputs.shape[1] // 4
        args.append(mask)
        in_specs.append(pl.BlockSpec((block, width), lambda i: (i, 0)))
        whole(inputs.T)
        whole(gating)
        outs.extend([jax.ShapeDtypeStruct((hidden, rows, width), jnp.bfloat16)] * 2)
        out_specs.extend([pl.BlockSpec((hidden, block, width), lambda i: (0, i, 0))] * 2)
        outs.append(jax.ShapeDtypeStruct(field.shape, jnp.float32))
        out_specs.append(line_spec)
    return pl.pallas_call(
        functools.partial(point_kernel, finish is not None, prepare is not None),
        grid=(rows // block,),
        in_specs=in_specs,
        out_specs=out_specs,
        out_shape=outs,
        scratch_shapes=[pltpu.VMEM((block * hidden, width), jnp.float32)] * 2,
        compiler_params=pltpu.CompilerParams(vmem_limit_bytes=40 * 2**20),
    )(*args)


def local(
    pair, token_mask, token_count, out_inputs, out_gating, out_final, in_inputs, in_gating, in_final
):
    height, width = pair.shape[:2]
    sizes = lax.axis_size("row"), lax.axis_size("col")
    positions = lax.iota(jnp.int32, token_mask.shape[0])
    valid = (token_mask * (positions < token_count[0]).astype(jnp.int32)).astype(jnp.float32)
    row_valid = lax.dynamic_slice_in_dim(valid, lax.axis_index("row") * height, height)
    col_valid = lax.dynamic_slice_in_dim(valid, lax.axis_index("col") * width, width)
    pmask = row_valid[:, None] * col_valid[None, :]
    a, b, gate = point(pair, prepare=(pmask, out_inputs, out_gating))
    tri = triangle(a, b, *sizes, True)
    middle, a, b, gate = point(pair, (tri, gate, out_final), (pmask, in_inputs, in_gating))
    tri = triangle(a, b, *sizes, False)
    return point(middle, finish=(tri, gate, in_final))[0]


def solution(mesh):
    tile = P(("groups", "row"), "col", None)
    in_specs = (tile, P("groups"), P("groups")) + (P(),) * 6
    return jax.shard_map(local, mesh=mesh, in_specs=in_specs, out_specs=tile, check_vma=False)
```

```python
import functools

import jax
import jax.numpy as jnp
from jax import lax
from jax.experimental import pallas as pl
from jax.experimental.pallas import tpu as pltpu
from jax.sharding import PartitionSpec as P

CHUNKS = 4


MESH = pl.DeviceIdType.MESH


def triangle_kernel(
    outgoing, chunks, rows, half_cols, a_hbm, b_hbm, o_hbm, a_in, b_in, t_out, a_full, b_full,
    a_send, a_recv, b_send, b_recv, t_send, t_recv, own_sem,
):
    members = rows * half_cols
    depth = a_in.shape[3]
    owned = depth * chunks
    height, width = a_in.shape[-2:]
    row, col = lax.axis_index("row"), lax.axis_index("col")
    half = lax.div(col, half_cols)
    mine = row * half_cols + lax.rem(col, half_cols)
    a_flips = 1 if outgoing else 2
    t_flips = 2 if outgoing else 1

    def side_of(flip):
        return half if flip == 0 else 1 - half

    def ahead(off):
        return lax.rem(mine + off, members)

    def behind(off):
        return lax.rem(mine + members - off, members)

    def place(flip, member):
        return {
            "row": lax.div(member, half_cols),
            "col": side_of(flip) * half_cols + lax.rem(member, half_cols),
        }

    def slots(count, flip):
        return side_of(flip) if count == 2 else 0

    def each(flips, body):
        for flip in reversed(range(flips)):
            first = 1 if flip == 0 else 0

            def one(off, carry, flip=flip):
                body(flip, off)
                return carry

            lax.fori_loop(first, members, one, 0)

    def inward(source, landing, send, recv, flips, q, flip, off, slot_side, slot_member):
        target = ahead(off)
        return pltpu.make_async_remote_copy(
            src_ref=source.at[pl.ds(target * owned + q * depth, depth)],
            dst_ref=landing.at[q, slot_side, slot_member],
            send_sem=send.at[q, flip, off],
            recv_sem=recv.at[q, flip, off],
            device_id=place(flip, target),
            device_id_type=MESH,
        )

    def outward(q, flip, off, o_side, o_member):
        target = ahead(off)
        return pltpu.make_async_remote_copy(
            src_ref=t_out.at[q, slots(t_flips, flip), target],
            dst_ref=o_hbm.at[o_side, pl.ds(o_member * owned + q * depth, depth)],
            send_sem=t_send.at[q, flip, off],
            recv_sem=t_recv.at[q, flip, off],
            device_id=place(flip, target),
            device_id_type=MESH,
        )

    operands = (
        (a_hbm, a_in, a_send, a_recv, a_flips),
        (b_hbm, b_in, b_send, b_recv, 1),
    )

    def local_in(which, q):
        source, landing, _, _, flips = operands[which]
        return pltpu.make_async_copy(
            source.at[pl.ds(mine * owned + q * depth, depth)],
            landing.at[q, slots(flips, 0), mine],
            own_sem.at[which, q],
        )

    def local_out(q):
        return pltpu.make_async_copy(
            t_out.at[q, slots(t_flips, 0), mine],
            o_hbm.at[slots(t_flips, 0), pl.ds(mine * owned + q * depth, depth)],
            own_sem.at[2, q],
        )

    def start_in(q):
        for which in range(2):
            source, landing, send, recv, flips = operands[which]
            each(
                flips,
                lambda flip, off: inward(
                    source, landing, send, recv, flips, q, flip, off, slots(flips, 0), mine
                ).start(),
            )
            local_in(which, q).start()

    def wait_in(q):
        for which in range(2):
            source, landing, send, recv, flips = operands[which]
            each(
                flips,
                lambda flip, off: inward(
                    source, landing, send, recv, flips, q, flip, off, slots(flips, flip), behind(off)
                ).wait_recv(),
            )
            local_in(which, q).wait()

    barrier = pltpu.get_barrier_semaphore()
    each(
        2,
        lambda flip, off: pl.semaphore_signal(
            barrier, inc=1, device_id=place(flip, ahead(off)), device_id_type=MESH
        ),
    )
    pl.semaphore_wait(barrier, 2 * members - 1)

    def fill(full, landing, q, channel, flips):
        for side in range(flips):
            for member in range(members):
                r = (member // half_cols) * height
                c = (side * half_cols + member % half_cols) * width
                full[r : r + height, c : c + width] = landing[q, side, member, channel]

    dims = (((1,), (1,)), ((), ())) if outgoing else (((0,), (0,)), ((), ()))

    ready = min(2, chunks)
    for q in range(ready):
        start_in(q)
    for q in range(chunks):
        wait_in(q)

        def multiply(channel, carry, q=q):
            fill(a_full, a_in, q, channel, a_flips)
            fill(b_full, b_in, q, channel, 1)
            tri = lax.dot_general(
                a_full[...], b_full[...], dims, preferred_element_type=jnp.float32
            ).astype(jnp.bfloat16)
            for side in range(t_flips):
                for member in range(members):
                    r = (member // half_cols) * height
                    c = (side * half_cols + member % half_cols) * width
                    t_out[q, side, member, channel] = tri[r : r + height, c : c + width]
            return carry

        lax.fori_loop(0, depth, multiply, 0)
        each(
            t_flips, lambda flip, off: outward(q, flip, off, slots(t_flips, 0), mine).start()
        )
        local_out(q).start()
        if q + ready < chunks:
            start_in(q + ready)
    for q in range(chunks):
        for which in range(2):
            source, landing, send, recv, flips = operands[which]
            each(
                flips,
                lambda flip, off: inward(
                    source, landing, send, recv, flips, q, flip, off, slots(flips, 0), mine
                ).wait_send(),
            )
        each(
            t_flips, lambda flip, off: outward(q, flip, off, slots(t_flips, 0), mine).wait_send()
        )
        each(
            t_flips,
            lambda flip, off: outward(q, flip, off, slots(t_flips, flip), behind(off)).wait_recv(),
        )
        local_out(q).wait()


def triangle(a, b, rows, cols, outgoing):
    hidden, height, width = a.shape
    half_cols = cols // 2
    members = rows * half_cols
    owned = hidden // members
    chunks = min(CHUNKS, owned)
    depth = owned // chunks
    n = rows * height
    a_flips, t_flips = (1, 2) if outgoing else (2, 1)

    def blocks(flips):
        return pltpu.VMEM((chunks, flips, members, depth, height, width), jnp.bfloat16)

    def sems(flips):
        return pltpu.SemaphoreType.DMA((chunks, flips, members))

    anywhere = pl.BlockSpec(memory_space=pl.ANY)
    return pl.pallas_call(
        functools.partial(triangle_kernel, outgoing, chunks, rows, half_cols),
        in_specs=[anywhere, anywhere],
        out_specs=anywhere,
        out_shape=jax.ShapeDtypeStruct((t_flips, hidden, height, width), jnp.bfloat16),
        scratch_shapes=[
            blocks(a_flips),
            blocks(1),
            blocks(t_flips),
            pltpu.VMEM((n, a_flips * half_cols * width), jnp.bfloat16),
            pltpu.VMEM((n, half_cols * width), jnp.bfloat16),
            sems(a_flips),
            sems(a_flips),
            sems(1),
            sems(1),
            sems(t_flips),
            sems(t_flips),
            pltpu.SemaphoreType.DMA((3, chunks)),
        ],
        compiler_params=pltpu.CompilerParams(
            collective_id=0 if outgoing else 1,
            has_side_effects=True,
            vmem_limit_bytes=48 * 2**20,
        ),
    )(a, b)


def layer_norm(x, axis):
    mean = jnp.mean(x, axis=axis, keepdims=True)
    centred = x - mean
    var = jnp.mean(centred * centred, axis=axis, keepdims=True)
    return centred * lax.rsqrt(var + 1e-05)


def sigmoid(x):
    return 0.5 * jnp.tanh(0.5 * x) + 0.5


def point_kernel(finishes, prepares, *refs):
    refs = list(refs)
    field_ref = refs.pop(0)
    height, width, channels = field_ref.shape
    if finishes:
        tri_ref, gate_ref, final_ref = refs.pop(0), refs.pop(0), refs.pop(0)
    if prepares:
        mask_ref, inputs_ref, gating_ref = refs.pop(0), refs.pop(0), refs.pop(0)
    if finishes:
        middle_ref = refs.pop(0)
    if prepares:
        a_ref, b_ref, new_gate_ref = refs.pop(0), refs.pop(0), refs.pop(0)
    one, two = refs

    if finishes:
        hidden = tri_ref.shape[1]
        for h in range(hidden):
            tri = tri_ref[0, h].astype(jnp.float32)
            for side in range(1, tri_ref.shape[0]):
                tri = tri + tri_ref[side, h].astype(jnp.float32)
            one[pl.ds(h, height, stride=hidden), :] = tri

    def line(i):
        field = field_ref[i].astype(jnp.float32)
        if finishes:
            at = slice(i * hidden, (i + 1) * hidden)
            value = lax.dot_general(
                layer_norm(one[at, :], 0).astype(jnp.bfloat16),
                final_ref[...],
                (((0,), (0,)), ((), ())),
                preferred_element_type=jnp.float32,
            )
            rounded = (field + gate_ref[i] * value).astype(jnp.bfloat16)
            middle_ref[i] = rounded
            field = rounded.astype(jnp.float32)
        if prepares:
            size = inputs_ref.shape[0] // 4
            normed = layer_norm(field, -1).astype(jnp.bfloat16)
            proj = lax.dot_general(
                inputs_ref[...], normed, (((1,), (1,)), ((), ())),
                preferred_element_type=jnp.float32,
            )
            mask = mask_ref[i : i + 1, :]
            at = slice(i * size, (i + 1) * size)
            one[at, :] = mask * sigmoid(proj[:size]) * proj[size : 2 * size]
            two[at, :] = mask * sigmoid(proj[2 * size : 3 * size]) * proj[3 * size :]
            new_gate_ref[i] = sigmoid(
                jnp.dot(normed, gating_ref[...], preferred_element_type=jnp.float32)
            )

    for i in range(height):
        line(i)
    if prepares:
        hidden = a_ref.shape[0]
        for h in range(hidden):
            rows = pl.ds(h, height, stride=hidden)
            a_ref[h] = one[rows, :].astype(jnp.bfloat16)
            b_ref[h] = two[rows, :].astype(jnp.bfloat16)


def point(field, finish=None, prepare=None):
    rows, width, channels = field.shape
    block = 16
    line_spec = pl.BlockSpec((block, width, channels), lambda i: (i, 0, 0))
    args, in_specs, outs, out_specs = [field], [line_spec], [], []

    def whole(array):
        args.append(array)
        in_specs.append(pl.BlockSpec(array.shape, lambda i: (0,) * array.ndim))

    if finish is not None:
        tri, gate, final = finish
        hidden = tri.shape[1]
        args.extend((tri, gate))
        in_specs.append(
            pl.BlockSpec((tri.shape[0], hidden, block, width), lambda i: (0, 0, i, 0))
        )
        in_specs.append(line_spec)
        whole(final)
        outs.append(jax.ShapeDtypeStruct(field.shape, jnp.bfloat16))
        out_specs.append(line_spec)
    if prepare is not None:
        mask, inputs, gating = prepare
        hidden = inputs.shape[1] // 4
        args.append(mask)
        in_specs.append(pl.BlockSpec((block, width), lambda i: (i, 0)))
        whole(inputs.T)
        whole(gating)
        outs.extend([jax.ShapeDtypeStruct((hidden, rows, width), jnp.bfloat16)] * 2)
        out_specs.extend([pl.BlockSpec((hidden, block, width), lambda i: (0, i, 0))] * 2)
        outs.append(jax.ShapeDtypeStruct(field.shape, jnp.float32))
        out_specs.append(line_spec)
    return pl.pallas_call(
        functools.partial(point_kernel, finish is not None, prepare is not None),
        grid=(rows // block,),
        in_specs=in_specs,
        out_specs=out_specs,
        out_shape=outs,
        scratch_shapes=[pltpu.VMEM((block * hidden, width), jnp.float32)] * 2,
        compiler_params=pltpu.CompilerParams(vmem_limit_bytes=40 * 2**20),
    )(*args)


def local(
    pair, token_mask, token_count, out_inputs, out_gating, out_final, in_inputs, in_gating, in_final
):
    height, width = pair.shape[:2]
    sizes = lax.axis_size("row"), lax.axis_size("col")
    positions = lax.iota(jnp.int32, token_mask.shape[0])
    valid = (token_mask * (positions < token_count[0]).astype(jnp.int32)).astype(jnp.float32)
    row_valid = lax.dynamic_slice_in_dim(valid, lax.axis_index("row") * height, height)
    col_valid = lax.dynamic_slice_in_dim(valid, lax.axis_index("col") * width, width)
    pmask = row_valid[:, None] * col_valid[None, :]
    a, b, gate = point(pair, prepare=(pmask, out_inputs, out_gating))
    tri = triangle(a, b, *sizes, True)
    middle = point(pair, finish=(tri, gate, out_final))[0]
    a, b, gate = point(middle, prepare=(pmask, in_inputs, in_gating))
    tri = triangle(a, b, *sizes, False)
    return point(middle, finish=(tri, gate, in_final))[0]


def solution(mesh):
    tile = P(("groups", "row"), "col", None)
    in_specs = (tile, P("groups"), P("groups")) + (P(),) * 6
    return jax.shard_map(local, mesh=mesh, in_specs=in_specs, out_specs=tile, check_vma=False)
```
